32 devices in a mesh: vrow: 16 (over z, y, core), vcol: 2 (over x).
Axes of the slice: x: 2, y: 2, z: 4, core: 2. Of those that a mesh axis runs over, the one named last changes fastest.
Arguments:
- pairs: int32 [64, 2], replicated, may hold values from 0 to 119, as said below
- offsets: int32 [2, 2], replicated, may hold values from 0 to 1016, as said below
- amplitudes: bfloat16 [64, 1024, 1024], P(None, 'vrow', 'vcol'), may hold values from -0.59765625 to 0.59765625
- slabs: bfloat16 [2, 2, 1024, 8, 2304], P(None, None, ('vrow', 'vcol')), may hold values from -0.86328125 to 0.86328125
Outputs:
- residual: float32 [64, 1024, 1024], P(None, 'vrow', 'vcol')
The draws below stay inside these ranges and needn't reach their ends.
Inputs may be any that keep to these rules, and one draw needn't show every extreme that they name: `pairs`: each row is an occupied pair i <= j; some rows have i = j. `offsets`: every offset is a multiple of 8.
All inputs are finite; a program needn't handle non-finite values.
Results may differ from the reference program's by a relative error of at most 0.0003.
Values may be sent and summed in bfloat16 or wider, within the bound.
A program may use at most 192 MiB of HBM per device.

```python
import jax
import jax.numpy as jnp
from jax import lax

NOCC = 120
V = 1024
Q = 2304
BLK = 8
P_SIZE = 64
STEPS = 2


def draw_pairs(key, part):
    key = jax.random.fold_in(key, 11)
    key_first, key_span, key_diag = jax.random.split(key, 3)
    first = jax.random.randint(key_first, (P_SIZE,), 0, NOCC)
    span = jax.random.randint(key_span, (P_SIZE,), 0, NOCC)
    second = first + jnp.remainder(span, NOCC - first)
    flag = jax.random.randint(key_diag, (P_SIZE,), 0, 4) == 0
    second = jnp.where(flag, first, second)
    first = first.at[0].set(0)
    second = second.at[0].set(NOCC - 1)
    second = second.at[1].set(first[1])
    return jnp.stack([first, second], axis=1).astype(jnp.int32)


def draw_offsets(key, part):
    key = jax.random.fold_in(key, 23)
    key_picks, key_place = jax.random.split(key, 2)
    picks = jax.random.randint(key_picks, (STEPS * 2,), 0, V // BLK)
    place = jax.random.randint(key_place, (), 0, STEPS * 2)
    slots = jnp.arange(STEPS * 2)
    picks = jnp.where(slots == place, V // BLK - 1, picks)
    return (picks * BLK).reshape(STEPS, 2).astype(jnp.int32)


def levels(rng, dims, shards, low, largest):
    def one(position, shards_of):
        heights = jax.random.uniform(jax.random.fold_in(jax.random.fold_in(rng, 6), position), (shards_of,), jnp.float32, low / len(shards), largest / len(shards))
        return jnp.repeat(jnp.exp(heights), dims[position] // shards_of).reshape((-1,) + (1,) * (len(dims) - position - 1))

    level = one(*shards[0])
    for cut in shards[1:]:
        level = level * one(*cut)
    return level


def scatter_about(stream_key, shape, scale, reach, cuts=(), held_as=jnp.bfloat16):
    values = jax.random.normal(stream_key, shape, jnp.float32) * scale
    if len(cuts) > 0:
        values = levels(stream_key, shape, cuts, -0.22, 0.18) * values
    return jnp.clip(values, min=-reach, max=reach).astype(held_as)


def setup_inputs(seed: int = 0) -> dict:
    keys = jax.random.split(jax.random.key(seed), 5)
    return {
        "pairs": draw_pairs(jax.random.fold_in(keys[4], 71), 0),
        "offsets": draw_offsets(jax.random.fold_in(keys[4], 71), 0),
        "amplitudes": scatter_about(keys[2], (P_SIZE, V, V), 0.1, 0.59765625, ((1, 16), (2, 2))),
        "slabs": scatter_about(keys[3], (STEPS, 2, V, BLK, Q), (Q ** -0.25), 0.86328125, ((2, 32),)),
    }


def reference(pairs, offsets, amplitudes, slabs):
    offdiag = (pairs[:, 0] != pairs[:, 1]).astype(jnp.float32)
    amp = amplitudes.astype(jnp.float32)
    zero = jnp.zeros((), jnp.int32)
    total = jnp.zeros((P_SIZE, V, V), jnp.float32)
    starts = (jnp.arange(V // 128) * 128).astype(jnp.int32)
    for k in range(STEPS):
        first = offsets[k, 0].astype(jnp.int32)
        second = offsets[k, 1].astype(jnp.int32)
        forward = lax.dynamic_slice(amp, (zero, first, second), (P_SIZE, BLK, BLK))
        mirror = jnp.transpose(lax.dynamic_slice(amp, (zero, second, first), (P_SIZE, BLK, BLK)), (0, 2, 1))
        plus = 0.5 * (forward + mirror)
        minus = 0.5 * (forward - mirror) * offdiag[:, None, None]
        upper = plus + minus
        lower = plus - minus
        cols_c = slabs[k, 0].reshape(V * BLK, Q)
        cols_d = slabs[k, 1].reshape(V * BLK, Q)

        def block(start):
            rows_c = lax.dynamic_slice_in_dim(slabs[k, 0], start, 128, 0).reshape(128 * BLK, Q)
            rows_d = lax.dynamic_slice_in_dim(slabs[k, 1], start, 128, 0).reshape(128 * BLK, Q)
            direct = lax.dot_general(rows_c, cols_d, (((1,), (1,)), ((), ())), preferred_element_type=jnp.float32).reshape(128, BLK, V, BLK)
            swapped = lax.dot_general(rows_d, cols_c, (((1,), (1,)), ((), ())), preferred_element_type=jnp.float32).reshape(128, BLK, V, BLK)
            term = jnp.einsum("acbd,pcd->pab", direct, upper, precision=lax.Precision.HIGHEST)
            return term + jnp.einsum("adbc,pcd->pab", swapped, lower, precision=lax.Precision.HIGHEST)

        parts = lax.map(block, starts)
        total = total + jnp.transpose(parts, (1, 0, 2, 3)).reshape(P_SIZE, V, V)
    return total
```

```python
import functools

import jax
import jax.numpy as jnp
from jax import lax
from jax.experimental import pallas as pl
from jax.experimental.pallas import tpu as pltpu
from jax.sharding import PartitionSpec as P

BLK = 8
P_SIZE = 64
STEPS = 2


def broadcast(block, axis, holder):
    block = jnp.where(lax.axis_index(axis) == holder, block, jnp.zeros_like(block))
    return lax.psum(block, axis)


def ladder_part(rows, upper, lower, piece):
    depth = rows.shape[-1]
    count_a = rows.shape[2]
    count_b = piece.shape[2]
    rows_c = rows[0, 0].reshape(count_a * BLK, depth)
    rows_d = rows[0, 1].reshape(count_a * BLK, depth)
    piece_c = piece[0, 0].reshape(count_b * BLK, depth)
    piece_d = piece[0, 1].reshape(count_b * BLK, depth)
    direct = lax.dot_general(
        rows_c, piece_d, (((1,), (1,)), ((), ())), preferred_element_type=jnp.float32
    ).reshape(count_a, BLK, count_b, BLK)
    swapped = lax.dot_general(
        rows_d, piece_c, (((1,), (1,)), ((), ())), preferred_element_type=jnp.float32
    ).reshape(count_a, BLK, count_b, BLK)
    term = jnp.einsum("acbd,pcd->pab", direct, upper[0], precision=lax.Precision.HIGHEST)
    term = term + jnp.einsum("adbc,pcd->pab", swapped, lower[0], precision=lax.Precision.HIGHEST)
    term = term[None]
    return term


def blocks_of(pairs, offsets, amplitudes):
    col_count = lax.axis_size("vcol")
    rows_loc = amplitudes.shape[1]
    cols_loc = amplitudes.shape[2]
    offdiag = (pairs[:, 0] != pairs[:, 1]).astype(jnp.float32)
    zero = jnp.zeros((), jnp.int32)
    upper_list = []
    lower_list = []
    for k in range(STEPS):
        first = offsets[k, 0]
        second = offsets[k, 1]
        own_forward = lax.dynamic_slice(
            amplitudes, (zero, first % rows_loc, second % cols_loc), (P_SIZE, BLK, BLK)
        )
        own_mirror = lax.dynamic_slice(
            amplitudes, (zero, second % rows_loc, first % cols_loc), (P_SIZE, BLK, BLK)
        )
        root_forward = first // rows_loc * col_count + second // cols_loc
        root_mirror = second // rows_loc * col_count + first // cols_loc
        forward = broadcast(own_forward, ("vrow", "vcol"), root_forward).astype(jnp.float32)
        mirror_raw = broadcast(own_mirror, ("vrow", "vcol"), root_mirror).astype(jnp.float32)
        mirror = jnp.transpose(mirror_raw, (0, 2, 1))
        plus = 0.5 * (forward + mirror)
        minus = 0.5 * (forward - mirror) * offdiag[:, None, None]
        upper_list.append(plus + minus)
        lower_list.append(plus - minus)
    return upper_list, lower_list


def on_device(pairs, offsets, amplitudes, slabs):
    row_count = lax.axis_size("vrow")
    col_count = lax.axis_size("vcol")
    rows_loc = amplitudes.shape[1]
    cols_loc = amplitudes.shape[2]
    upper_list, lower_list = blocks_of(pairs, offsets, amplitudes)
    results = None
    for k in range(STEPS):
        rows = lax.all_gather(slabs[k], "vcol", axis=1, tiled=True)

        def single(piece, start, rows=rows, k=k):
            return ladder_part(rows[None], upper_list[k][None], lower_list[k][None], piece[None])

        term = single(lax.all_gather(slabs[k], "vrow", axis=1, tiled=True), jnp.int32(0))
        results = term if results is None else results + term
    groups = row_count // col_count
    inner = cols_loc // row_count
    shaped = results[0].reshape(P_SIZE, rows_loc, col_count, groups, 1, inner)
    moved = lax.all_to_all(shaped, "vcol", split_axis=2, concat_axis=4, tiled=True)
    combined = moved.reshape(P_SIZE, rows_loc, cols_loc)
    return combined


MESH = pl.DeviceIdType.MESH
LANES = 128
PAIRS = ((1, 4), (2, 5), (3, 6), (0, 7))
BEHIND = (0, 1, 2, 3, 7)
AHEAD = (0, 4, 5, 6, 7)
FORWARD = ((0, 0), (0, 1), (1, 0), (1, 1), (2, 0), (2, 1), (3, 0))
BACKWARD = ((0, 1), (0, 0), (1, 1), (1, 0), (2, 1), (2, 0), (3, 1))


def ring_place(row):
    y = lax.rem(row // 2, 2)
    z = row // 4
    return z + y * (7 - 2 * z)


def ring_row(place, core):
    y = place // 4
    z = place + y * (7 - 2 * place)
    return z * 4 + y * 2 + core


def ring_kernel(
    weights, natural, turned, gathered, mine, theirs,
    rows, piece, factor, totals,
    f_send, f_recv, b_send, b_recv, s_send, s_recv, a_send, a_recv, o_send, o_recv, l_sem, p_sem, t_sem,
):
    row = lax.axis_index("vrow")
    col = lax.axis_index("vcol")
    core = lax.rem(row, 2)
    place = ring_place(row)
    right = (ring_row(lax.rem(place + 1, 8), core), col)
    left = (ring_row(lax.rem(place + 7, 8), core), col)
    sibling = (row + 1 - 2 * core, col)
    partner = (row, 1 - col)

    barrier = pltpu.get_barrier_semaphore()
    for other in (right, left, sibling, partner):
        pl.semaphore_signal(barrier, inc=1, device_id=other, device_id_type=MESH)
    pl.semaphore_wait(barrier, 4)

    def remote(src, dst, send, recv, target):
        return pltpu.make_async_remote_copy(
            src_ref=src, dst_ref=dst, send_sem=send, recv_sem=recv, device_id=target, device_id_type=MESH
        )

    def hop(order, slots, send, recv, target, i):
        step, k = order[i]
        src = turned.at[k] if step == 0 else gathered.at[slots[step], core, k]
        return remote(src, gathered.at[slots[step + 1], core, k], send.at[i], recv.at[i], target)

    forward = [hop(FORWARD, BEHIND, f_send, f_recv, right, i) for i in range(7)]
    backward = [hop(BACKWARD, AHEAD, b_send, b_recv, left, i) for i in range(7)]

    def share(slot, k):
        src = turned.at[k] if slot == 0 else gathered.at[slot, core, k]
        return remote(src, gathered.at[slot, core, k], s_send.at[slot, k], s_recv.at[slot, k], sibling)

    shares = {(slot, k): share(slot, k) for slot in range(8) for k in range(2)}
    width = natural.shape[2]
    a_copy = remote(natural, rows.at[:, :, pl.ds(col * width, width), :], a_send, a_recv, partner)
    a_own = pltpu.make_async_copy(natural, rows.at[:, :, pl.ds(col * width, width), :], l_sem.at[0])
    own = pltpu.make_async_copy(turned, gathered.at[0, core], l_sem.at[1])

    for i in range(2):
        forward[i].start()
        backward[i].start()
    a_copy.start()
    own.start()
    a_own.start()
    for k in range(2):
        shares[0, k].start()

    outs = [remote(totals.at[u], theirs.at[u], o_send.at[u], o_recv.at[u], partner) for u in range(4)]
    keeps = [pltpu.make_async_copy(totals.at[u], mine.at[u], t_sem.at[u]) for u in range(4)]
    count = rows.shape[2] // BLK
    shard = turned.shape[3]

    def compute(u):
        loads = []
        for e, slot in enumerate(PAIRS[u]):
            for c in range(2):
                for k in range(2):
                    dst = piece.at[k, :, :, pl.ds((e * 2 + c) * shard, shard), :]
                    loads.append(pltpu.make_async_copy(gathered.at[slot, c, k], dst, p_sem.at[e, c, k]))
        for load in loads:
            load.start()
        for load in loads:
            load.wait()

        def products(i, carry):
            k = i // 8
            t = lax.rem(i // 4, 2)
            d = lax.rem(i, 4)
            cols = piece[k, 1 - t, pl.ds(d * 2, 2)].reshape(2 * LANES, piece.shape[-1])
            part = lax.dot_general(
                rows[k, t], cols, (((1,), (1,)), ((), ())), preferred_element_type=jnp.float32
            ).reshape(count, BLK, 2 * LANES)
            part = jnp.concatenate([part[:, :, :LANES], part[:, :, LANES:]], axis=1)
            high = part.astype(jnp.bfloat16)
            low = (part - high.astype(jnp.float32)).astype(jnp.bfloat16)
            at = k * 256 + t * 128 + d * 16
            factor[:, pl.ds(pl.multiple_of(at, 16), 16), :] = high
            factor[:, pl.ds(pl.multiple_of(at + 64, 16), 16), :] = low
            return carry

        lax.fori_loop(0, 16, products, 0)

        def contract(a, carry):
            res = jnp.dot(weights[...], factor[a], preferred_element_type=jnp.float32)
            totals[u, pl.ds(a, P_SIZE, stride=count), :] = res[:P_SIZE] + res[P_SIZE:]
            return carry

        lax.fori_loop(0, count, contract, 0)
        outs[u].start()
        keeps[u].start()

    def sibling_here(slots):
        for slot in slots:
            for k in range(2):
                shares[slot, k].wait_recv()

    for i in range(7):
        forward[i].wait_recv()
        if i + 2 < 7:
            forward[i + 2].start()
        step, k = FORWARD[i]
        shares[BEHIND[step + 1], k].start()
        backward[i].wait_recv()
        if i + 2 < 7:
            backward[i + 2].start()
        step, k = BACKWARD[i]
        shares[AHEAD[step + 1], k].start()
        if i == 1:
            a_own.wait()
            a_copy.wait_recv()
        if i in (1, 3, 5):
            u = i // 2
            sibling_here(PAIRS[u])
            compute(u)
    own.wait()
    sibling_here(PAIRS[3])
    compute(3)
    for copy in forward + backward + list(shares.values()) + [a_copy]:
        copy.wait_send()
    for u in range(4):
        keeps[u].wait()
        outs[u].wait()


def place_kernel(table, mine, theirs, out):
    i = pl.program_id(0)
    half = table[4 + i]
    swap = table[8]
    a = mine[0]
    b = theirs[0]
    first = jnp.where(swap == 0, a, b)
    second = jnp.where(swap == 0, b, a)
    first = jnp.where(half == 0, first[:, :, :64], first[:, :, 64:])
    second = jnp.where(half == 0, second[:, :, :64], second[:, :, 64:])
    out[...] = jnp.concatenate(
        [first[:, :, :32], second[:, :, :32], first[:, :, 32:], second[:, :, 32:]], axis=-1
    )


def ladder_weights(pairs, offsets, amplitudes):
    uppers, lowers = blocks_of(pairs, offsets, amplitudes)
    parts = []
    for k in range(STEPS):
        up = jnp.transpose(uppers[k], (0, 2, 1)).reshape(P_SIZE, BLK * BLK)
        low = lowers[k].reshape(P_SIZE, BLK * BLK)
        parts.extend([up, up, low, low])
    full = jnp.concatenate(parts, axis=1)
    high = lax.reduce_precision(full, exponent_bits=8, mantissa_bits=7)
    return jnp.concatenate([high, full - high], axis=0).astype(jnp.bfloat16)


def on_plane(pairs, offsets, amplitudes, slabs):
    shard, depth = slabs.shape[2], slabs.shape[4]
    rows_loc, cols_loc = amplitudes.shape[1], amplitudes.shape[2]
    weights = ladder_weights(pairs, offsets, amplitudes)
    natural = slabs.reshape(STEPS, 2, shard * BLK, depth)
    turned = jnp.swapaxes(slabs, 2, 3)
    bf16, f32 = jnp.bfloat16, jnp.float32
    dma = pltpu.SemaphoreType.DMA
    anywhere = pl.BlockSpec(memory_space=pl.ANY)
    _, mine, theirs = pl.pallas_call(
        ring_kernel,
        out_shape=(
            jax.ShapeDtypeStruct((8, 2, STEPS, 2, BLK, shard, depth), bf16),
            jax.ShapeDtypeStruct((4, P_SIZE * rows_loc, LANES), f32),
            jax.ShapeDtypeStruct((4, P_SIZE * rows_loc, LANES), f32),
        ),
        in_specs=[pl.BlockSpec(memory_space=pltpu.VMEM), anywhere, anywhere],
        out_specs=(anywhere, anywhere, anywhere),
        scratch_shapes=[
            pltpu.VMEM((STEPS, 2, rows_loc * BLK, depth), bf16),
            pltpu.VMEM((STEPS, 2, BLK, LANES, depth), bf16),
            pltpu.VMEM((rows_loc, STEPS * 256, LANES), bf16),
            pltpu.VMEM((4, P_SIZE * rows_loc, LANES), f32),
            dma((7,)), dma((7,)), dma((7,)), dma((7,)), dma((8, 2)), dma((8, 2)),
            dma, dma, dma((4,)), dma((4,)), dma((2,)), dma((2, 2, 2)), dma((4,)),
        ],
        compiler_params=pltpu.CompilerParams(
            collective_id=0, has_side_effects=True, vmem_limit_bytes=60 * 1024 * 1024
        ),
        name="ladder_ring",
    )(weights, natural, turned)
    row = lax.axis_index("vrow")
    col = lax.axis_index("vcol")
    chip = jnp.arange(4, dtype=jnp.int32)
    z = 2 * col + chip // 2
    y = chip % 2
    rel = (z + y * (7 - 2 * z) - ring_place(row)) % 8
    block = jnp.array([3, 0, 1, 2, 3, 2, 1, 0], jnp.int32)[rel]
    half = jnp.array([0, 1, 1, 1, 1, 0, 0, 0], jnp.int32)[rel]
    table = jnp.concatenate([block, half, col[None].astype(jnp.int32)])
    chunk = 16
    source = pl.BlockSpec((1, chunk, rows_loc, LANES), lambda i, j, t: (t[i], j, 0, 0))
    return pl.pallas_call(
        place_kernel,
        grid_spec=pltpu.PrefetchScalarGridSpec(
            num_scalar_prefetch=1,
            grid=(4, P_SIZE // chunk),
            in_specs=[source, source],
            out_specs=pl.BlockSpec((chunk, rows_loc, LANES), lambda i, j, t: (j, 0, i)),
        ),
        out_shape=jax.ShapeDtypeStruct((P_SIZE, rows_loc, cols_loc), f32),
        name="ladder_place",
    )(table, mine.reshape(4, P_SIZE, rows_loc, LANES), theirs.reshape(4, P_SIZE, rows_loc, LANES))


def solution(mesh):
    in_specs = (P(), P(), P(None, "vrow", "vcol"), P(None, None, ("vrow", "vcol"), None, None))
    out_specs = P(None, "vrow", "vcol")
    on_slice = on_plane if (mesh.shape["vrow"], mesh.shape["vcol"]) == (16, 2) else on_device
    return jax.shard_map(
        on_slice, mesh=mesh, in_specs=in_specs, out_specs=out_specs, check_vma=False
    )
```

```python
import functools

import jax
import jax.numpy as jnp
from jax import lax
from jax.experimental import pallas as pl
from jax.experimental.pallas import tpu as pltpu
from jax.sharding import PartitionSpec as P

BLK = 8
P_SIZE = 64
STEPS = 2


def broadcast(block, axis, holder):
    block = jnp.where(lax.axis_index(axis) == holder, block, jnp.zeros_like(block))
    return lax.psum(block, axis)


def ladder_part(rows, upper, lower, piece):
    depth = rows.shape[-1]
    count_a = rows.shape[2]
    count_b = piece.shape[2]
    rows_c = rows[0, 0].reshape(count_a * BLK, depth)
    rows_d = rows[0, 1].reshape(count_a * BLK, depth)
    piece_c = piece[0, 0].reshape(count_b * BLK, depth)
    piece_d = piece[0, 1].reshape(count_b * BLK, depth)
    direct = lax.dot_general(
        rows_c, piece_d, (((1,), (1,)), ((), ())), preferred_element_type=jnp.float32
    ).reshape(count_a, BLK, count_b, BLK)
    swapped = lax.dot_general(
        rows_d, piece_c, (((1,), (1,)), ((), ())), preferred_element_type=jnp.float32
    ).reshape(count_a, BLK, count_b, BLK)
    term = jnp.einsum("acbd,pcd->pab", direct, upper[0], precision=lax.Precision.HIGHEST)
    term = term + jnp.einsum("adbc,pcd->pab", swapped, lower[0], precision=lax.Precision.HIGHEST)
    term = term[None]
    return term


def blocks_of(pairs, offsets, amplitudes):
    col_count = lax.axis_size("vcol")
    rows_loc = amplitudes.shape[1]
    cols_loc = amplitudes.shape[2]
    offdiag = (pairs[:, 0] != pairs[:, 1]).astype(jnp.float32)
    zero = jnp.zeros((), jnp.int32)
    upper_list = []
    lower_list = []
    for k in range(STEPS):
        first = offsets[k, 0]
        second = offsets[k, 1]
        own_forward = lax.dynamic_slice(
            amplitudes, (zero, first % rows_loc, second % cols_loc), (P_SIZE, BLK, BLK)
        )
        own_mirror = lax.dynamic_slice(
            amplitudes, (zero, second % rows_loc, first % cols_loc), (P_SIZE, BLK, BLK)
        )
        root_forward = first // rows_loc * col_count + second // cols_loc
        root_mirror = second // rows_loc * col_count + first // cols_loc
        forward = broadcast(own_forward, ("vrow", "vcol"), root_forward).astype(jnp.float32)
        mirror_raw = broadcast(own_mirror, ("vrow", "vcol"), root_mirror).astype(jnp.float32)
        mirror = jnp.transpose(mirror_raw, (0, 2, 1))
        plus = 0.5 * (forward + mirror)
        minus = 0.5 * (forward - mirror) * offdiag[:, None, None]
        upper_list.append(plus + minus)
        lower_list.append(plus - minus)
    return upper_list, lower_list


def on_device(pairs, offsets, amplitudes, slabs):
    row_count = lax.axis_size("vrow")
    col_count = lax.axis_size("vcol")
    rows_loc = amplitudes.shape[1]
    cols_loc = amplitudes.shape[2]
    upper_list, lower_list = blocks_of(pairs, offsets, amplitudes)
    results = None
    for k in range(STEPS):
        rows = lax.all_gather(slabs[k], "vcol", axis=1, tiled=True)

        def single(piece, start, rows=rows, k=k):
            return ladder_part(rows[None], upper_list[k][None], lower_list[k][None], piece[None])

        term = single(lax.all_gather(slabs[k], "vrow", axis=1, tiled=True), jnp.int32(0))
        results = term if results is None else results + term
    groups = row_count // col_count
    inner = cols_loc // row_count
    shaped = results[0].reshape(P_SIZE, rows_loc, col_count, groups, 1, inner)
    moved = lax.all_to_all(shaped, "vcol", split_axis=2, concat_axis=4, tiled=True)
    combined = moved.reshape(P_SIZE, rows_loc, cols_loc)
    return combined


MESH = pl.DeviceIdType.MESH
LANES = 128
PAIRS = ((1, 4), (2, 5), (3, 6), (0, 7))
BEHIND = (0, 1, 2, 3, 7)
AHEAD = (0, 4, 5, 6, 7)
FORWARD = ((0, 0), (0, 1), (1, 0), (1, 1), (2, 0), (2, 1), (3, 0))
BACKWARD = ((0, 1), (0, 0), (1, 1), (1, 0), (2, 1), (2, 0), (3, 1))


def ring_place(row):
    y = lax.rem(row // 2, 2)
    z = row // 4
    return z + y * (7 - 2 * z)


def ring_row(place, core):
    y = place // 4
    z = place + y * (7 - 2 * place)
    return z * 4 + y * 2 + core


def ring_kernel(
    own_blocks, sides, natural, turned, gathered, mine, theirs,
    rows, piece, factor, totals, weights, sums, came, packed, x_send, x_recv,
    f_send, f_recv, b_send, b_recv, s_send, s_recv, a_send, a_recv, o_send, o_recv, l_sem, p_sem, t_sem,
):
    row = lax.axis_index("vrow")
    col = lax.axis_index("vcol")
    core = lax.rem(row, 2)
    place = ring_place(row)
    right = (ring_row(lax.rem(place + 1, 8), core), col)
    left = (ring_row(lax.rem(place + 7, 8), core), col)
    sibling = (row + 1 - 2 * core, col)
    partner = (row, 1 - col)

    barrier = pltpu.get_barrier_semaphore()
    flips = [sibling, partner]
    for bit in (2, 4, 8):
        flips.append((row + bit - 2 * bit * lax.rem(row // bit, 2), col))
    for other in [right, left] + flips:
        pl.semaphore_signal(barrier, inc=1, device_id=other, device_id_type=MESH)
    pl.semaphore_wait(barrier, 7)

    def remote(src, dst, send, recv, target):
        return pltpu.make_async_remote_copy(
            src_ref=src, dst_ref=dst, send_sem=send, recv_sem=recv, device_id=target, device_id_type=MESH
        )

    def hop(order, slots, send, recv, target, i):
        step, k = order[i]
        src = turned.at[k] if step == 0 else gathered.at[slots[step], core, k]
        return remote(src, gathered.at[slots[step + 1], core, k], send.at[i], recv.at[i], target)

    forward = [hop(FORWARD, BEHIND, f_send, f_recv, right, i) for i in range(7)]
    backward = [hop(BACKWARD, AHEAD, b_send, b_recv, left, i) for i in range(7)]

    def share(slot, k):
        src = turned.at[k] if slot == 0 else gathered.at[slot, core, k]
        return remote(src, gathered.at[slot, core, k], s_send.at[slot, k], s_recv.at[slot, k], sibling)

    shares = {(slot, k): share(slot, k) for slot in range(8) for k in range(2)}
    width = natural.shape[2]
    a_copy = remote(natural, rows.at[:, :, pl.ds(col * width, width), :], a_send, a_recv, partner)
    a_own = pltpu.make_async_copy(natural, rows.at[:, :, pl.ds(col * width, width), :], l_sem.at[0])
    own = pltpu.make_async_copy(turned, gathered.at[0, core], l_sem.at[1])

    sums[0] = own_blocks[...]
    for i, other in enumerate(flips):
        swap = remote(sums.at[i], came.at[i], x_send.at[i], x_recv.at[i], other)
        swap.start()
        swap.wait()
        sums[i + 1] = sums[i] + came[i]

    for i in range(2):
        forward[i].start()
        backward[i].start()
    a_copy.start()
    own.start()
    a_own.start()
    for k in range(2):
        shares[0, k].start()

    ahead = sums[5, 0].astype(jnp.float32)
    mirror = sums[5, 1].astype(jnp.float32)
    full = 0.5 * (ahead + mirror) + 0.5 * (ahead - mirror) * sides[...]
    high = full.astype(jnp.bfloat16)
    weights[:P_SIZE] = high
    weights[P_SIZE:] = (full - high.astype(jnp.float32)).astype(jnp.bfloat16)

    outs = [remote(totals.at[u], theirs.at[u], o_send.at[u], o_recv.at[u], partner) for u in range(3)]
    outs.append(remote(packed, theirs.at[3, pl.ds(0, packed.shape[0])], o_send.at[3], o_recv.at[3], partner))
    send_last = row // 8 == col
    keeps = [pltpu.make_async_copy(totals.at[u], mine.at[u], t_sem.at[u]) for u in range(4)]
    count = rows.shape[2] // BLK
    shard = turned.shape[3]

    def compute(u):
        loads = []
        for e, slot in enumerate(PAIRS[u]):
            for c in range(2):
                for k in range(2):
                    dst = piece.at[k, :, :, pl.ds((e * 2 + c) * shard, shard), :]
                    loads.append(pltpu.make_async_copy(gathered.at[slot, c, k], dst, p_sem.at[e, c, k]))
        for load in loads:
            load.start()
        for load in loads:
            load.wait()

        def products(i, carry):
            k = i // 8
            t = lax.rem(i // 4, 2)
            d = lax.rem(i, 4)
            cols = piece[k, 1 - t, pl.ds(d * 2, 2)].reshape(2 * LANES, piece.shape[-1])
            part = lax.dot_general(
                rows[k, t], cols, (((1,), (1,)), ((), ())), preferred_element_type=jnp.float32
            ).reshape(count, BLK, 2 * LANES)
            part = jnp.concatenate([part[:, :, :LANES], part[:, :, LANES:]], axis=1)
            high = part.astype(jnp.bfloat16)
            low = (part - high.astype(jnp.float32)).astype(jnp.bfloat16)
            at = k * 256 + t * 128 + d * 16
            factor[:, pl.ds(pl.multiple_of(at, 16), 16), :] = high
            factor[:, pl.ds(pl.multiple_of(at + 64, 16), 16), :] = low
            return carry

        lax.fori_loop(0, 16, products, 0)

        def contract(a, carry):
            res = jnp.dot(weights[...], factor[a], preferred_element_type=jnp.float32)
            res = res[:P_SIZE] + res[P_SIZE:]
            totals[u, pl.ds(a, P_SIZE, stride=count), :] = res
            if u == 3:
                moved = pltpu.roll(res, 64, 1)
                half = P_SIZE // 2
                low = lax.broadcasted_iota(jnp.int32, (half, LANES), 1) < 64
                opposite = jnp.where(low, moved[:half], res[half:])
                near = jnp.where(low, res[:half], moved[half:])
                packed[pl.ds(a, half, stride=count), :] = jnp.where(send_last, opposite, near)
            return carry

        lax.fori_loop(0, count, contract, 0)
        outs[u].start()
        keeps[u].start()

    def sibling_here(slots):
        for slot in slots:
            for k in range(2):
                shares[slot, k].wait_recv()

    for i in range(7):
        forward[i].wait_recv()
        if i + 2 < 7:
            forward[i + 2].start()
        step, k = FORWARD[i]
        shares[BEHIND[step + 1], k].start()
        backward[i].wait_recv()
        if i + 2 < 7:
            backward[i + 2].start()
        step, k = BACKWARD[i]
        shares[AHEAD[step + 1], k].start()
        if i == 1:
            a_own.wait()
            a_copy.wait_recv()
        if i in (1, 3, 5):
            u = i // 2
            sibling_here(PAIRS[u])
            compute(u)
    own.wait()
    sibling_here(PAIRS[3])
    compute(3)
    for copy in forward + backward + list(shares.values()) + [a_copy]:
        copy.wait_send()
    for u in range(4):
        keeps[u].wait()
        outs[u].wait()


def place_kernel(table, mine, theirs, out):
    i = pl.program_id(0)
    half = table[4 + i]
    other_half = jnp.where(table[i] == 3, pl.program_id(1) // 2, half)
    swap = table[8]
    a = mine[0]
    b = theirs[0]
    a = jnp.where(half == 0, a[:, :, :64], a[:, :, 64:])
    b = jnp.where(other_half == 0, b[:, :, :64], b[:, :, 64:])
    first = jnp.where(swap == 0, a, b)
    second = jnp.where(swap == 0, b, a)
    out[...] = jnp.concatenate(
        [first[:, :, :32], second[:, :, :32], first[:, :, 32:], second[:, :, 32:]], axis=-1
    )


def ladder_blocks(pairs, offsets, amplitudes):
    rows_loc, cols_loc = amplitudes.shape[1], amplitudes.shape[2]
    here = lax.axis_index(("vrow", "vcol"))
    col_count = lax.axis_size("vcol")
    zero = jnp.zeros((), jnp.int32)

    def own(first, second):
        block = lax.dynamic_slice(
            amplitudes, (zero, first % rows_loc, second % cols_loc), (P_SIZE, BLK, BLK)
        )
        root = first // rows_loc * col_count + second // cols_loc
        return jnp.where(here == root, block, jnp.zeros_like(block))

    def both(block_cd):
        cd = block_cd.reshape(P_SIZE, BLK * BLK)
        dc = jnp.transpose(block_cd, (0, 2, 1)).reshape(P_SIZE, BLK * BLK)
        return [dc, dc, cd, cd]

    ahead, mirror = [], []
    for k in range(STEPS):
        ahead.extend(both(own(offsets[k, 0], offsets[k, 1])))
        mirror.extend(both(jnp.transpose(own(offsets[k, 1], offsets[k, 0]), (0, 2, 1))))
    blocks = jnp.stack([jnp.concatenate(ahead, axis=1), jnp.concatenate(mirror, axis=1)])
    offdiag = (pairs[:, 0] != pairs[:, 1]).astype(jnp.float32)
    sign = 1.0 - 2.0 * (jnp.arange(blocks.shape[2]) // 128 % 2).astype(jnp.float32)
    return blocks, offdiag[:, None] * sign[None, :]


def on_plane(pairs, offsets, amplitudes, slabs):
    shard, depth = slabs.shape[2], slabs.shape[4]
    rows_loc, cols_loc = amplitudes.shape[1], amplitudes.shape[2]
    own_blocks, sides = ladder_blocks(pairs, offsets, amplitudes)
    natural = slabs.reshape(STEPS, 2, shard * BLK, depth)
    turned = jnp.swapaxes(slabs, 2, 3)
    bf16, f32 = jnp.bfloat16, jnp.float32
    dma = pltpu.SemaphoreType.DMA
    anywhere = pl.BlockSpec(memory_space=pl.ANY)
    _, mine, theirs = pl.pallas_call(
        ring_kernel,
        out_shape=(
            jax.ShapeDtypeStruct((8, 2, STEPS, 2, BLK, shard, depth), bf16),
            jax.ShapeDtypeStruct((4, P_SIZE * rows_loc, LANES), f32),
            jax.ShapeDtypeStruct((4, P_SIZE * rows_loc, LANES), f32),
        ),
        in_specs=[pl.BlockSpec(memory_space=pltpu.VMEM)] * 2 + [anywhere, anywhere],
        out_specs=(anywhere, anywhere, anywhere),
        scratch_shapes=[
            pltpu.VMEM((STEPS, 2, rows_loc * BLK, depth), bf16),
            pltpu.VMEM((STEPS, 2, BLK, LANES, depth), bf16),
            pltpu.VMEM((rows_loc, STEPS * 256, LANES), bf16),
            pltpu.VMEM((4, P_SIZE * rows_loc, LANES), f32),
            pltpu.VMEM((2 * P_SIZE, STEPS * 256), bf16),
            pltpu.VMEM((6, 2, P_SIZE, STEPS * 256), bf16),
            pltpu.VMEM((5, 2, P_SIZE, STEPS * 256), bf16),
            pltpu.VMEM((P_SIZE // 2 * rows_loc, LANES), f32),
            dma((5,)), dma((5,)),
            dma((7,)), dma((7,)), dma((7,)), dma((7,)), dma((8, 2)), dma((8, 2)),
            dma, dma, dma((4,)), dma((4,)), dma((2,)), dma((2, 2, 2)), dma((4,)),
        ],
        compiler_params=pltpu.CompilerParams(
            collective_id=0, has_side_effects=True, vmem_limit_bytes=60 * 1024 * 1024
        ),
        name="ladder_ring",
    )(own_blocks, sides, natural, turned)
    row = lax.axis_index("vrow")
    col = lax.axis_index("vcol")
    chip = jnp.arange(4, dtype=jnp.int32)
    z = 2 * col + chip // 2
    y = chip % 2
    rel = (z + y * (7 - 2 * z) - ring_place(row)) % 8
    block = jnp.array([3, 0, 1, 2, 3, 2, 1, 0], jnp.int32)[rel]
    half = jnp.array([0, 1, 1, 1, 1, 0, 0, 0], jnp.int32)[rel]
    table = jnp.concatenate([block, half, col[None].astype(jnp.int32)])
    chunk = 16
    source = pl.BlockSpec((1, chunk, rows_loc, LANES), lambda i, j, t: (t[i], j, 0, 0))
    other = pl.BlockSpec(
        (1, chunk, rows_loc, LANES), lambda i, j, t: (t[i], jnp.where(t[i] == 3, j % 2, j), 0, 0)
    )
    return pl.pallas_call(
        place_kernel,
        grid_spec=pltpu.PrefetchScalarGridSpec(
            num_scalar_prefetch=1,
            grid=(4, P_SIZE // chunk),
            in_specs=[source, other],
            out_specs=pl.BlockSpec((chunk, rows_loc, LANES), lambda i, j, t: (j, 0, i)),
        ),
        out_shape=jax.ShapeDtypeStruct((P_SIZE, rows_loc, cols_loc), f32),
        name="ladder_place",
    )(table, mine.reshape(4, P_SIZE, rows_loc, LANES), theirs.reshape(4, P_SIZE, rows_loc, LANES))


def solution(mesh):
    in_specs = (P(), P(), P(None, "vrow", "vcol"), P(None, None, ("vrow", "vcol"), None, None))
    out_specs = P(None, "vrow", "vcol")
    on_slice = on_plane if (mesh.shape["vrow"], mesh.shape["vcol"]) == (16, 2) else on_device
    return jax.shard_map(
        on_slice, mesh=mesh, in_specs=in_specs, out_specs=out_specs, check_vma=False
    )
```

```python
import functools

import jax
import jax.numpy as jnp
from jax import lax
from jax.experimental import pallas as pl
from jax.experimental.pallas import tpu as pltpu
from jax.sharding import PartitionSpec as P

BLK = 8
P_SIZE = 64
STEPS = 2


def broadcast(block, axis, holder):
    block = jnp.where(lax.axis_index(axis) == holder, block, jnp.zeros_like(block))
    return lax.psum(block, axis)


def ladder_part(rows, upper, lower, piece):
    depth = rows.shape[-1]
    count_a = rows.shape[2]
    count_b = piece.shape[2]
    rows_c = rows[0, 0].reshape(count_a * BLK, depth)
    rows_d = rows[0, 1].reshape(count_a * BLK, depth)
    piece_c = piece[0, 0].reshape(count_b * BLK, depth)
    piece_d = piece[0, 1].reshape(count_b * BLK, depth)
    direct = lax.dot_general(
        rows_c, piece_d, (((1,), (1,)), ((), ())), preferred_element_type=jnp.float32
    ).reshape(count_a, BLK, count_b, BLK)
    swapped = lax.dot_general(
        rows_d, piece_c, (((1,), (1,)), ((), ())), preferred_element_type=jnp.float32
    ).reshape(count_a, BLK, count_b, BLK)
    term = jnp.einsum("acbd,pcd->pab", direct, upper[0], precision=lax.Precision.HIGHEST)
    term = term + jnp.einsum("adbc,pcd->pab", swapped, lower[0], precision=lax.Precision.HIGHEST)
    term = term[None]
    return term


def blocks_of(pairs, offsets, amplitudes):
    col_count = lax.axis_size("vcol")
    rows_loc = amplitudes.shape[1]
    cols_loc = amplitudes.shape[2]
    offdiag = (pairs[:, 0] != pairs[:, 1]).astype(jnp.float32)
    zero = jnp.zeros((), jnp.int32)
    upper_list = []
    lower_list = []
    for k in range(STEPS):
        first = offsets[k, 0]
        second = offsets[k, 1]
        own_forward = lax.dynamic_slice(
            amplitudes, (zero, first % rows_loc, second % cols_loc), (P_SIZE, BLK, BLK)
        )
        own_mirror = lax.dynamic_slice(
            amplitudes, (zero, second % rows_loc, first % cols_loc), (P_SIZE, BLK, BLK)
        )
        root_forward = first // rows_loc * col_count + second // cols_loc
        root_mirror = second // rows_loc * col_count + first // cols_loc
        forward = broadcast(own_forward, ("vrow", "vcol"), root_forward).astype(jnp.float32)
        mirror_raw = broadcast(own_mirror, ("vrow", "vcol"), root_mirror).astype(jnp.float32)
        mirror = jnp.transpose(mirror_raw, (0, 2, 1))
        plus = 0.5 * (forward + mirror)
        minus = 0.5 * (forward - mirror) * offdiag[:, None, None]
        upper_list.append(plus + minus)
        lower_list.append(plus - minus)
    return upper_list, lower_list


def on_device(pairs, offsets, amplitudes, slabs):
    row_count = lax.axis_size("vrow")
    col_count = lax.axis_size("vcol")
    rows_loc = amplitudes.shape[1]
    cols_loc = amplitudes.shape[2]
    upper_list, lower_list = blocks_of(pairs, offsets, amplitudes)
    results = None
    for k in range(STEPS):
        rows = lax.all_gather(slabs[k], "vcol", axis=1, tiled=True)

        def single(piece, start, rows=rows, k=k):
            return ladder_part(rows[None], upper_list[k][None], lower_list[k][None], piece[None])

        term = single(lax.all_gather(slabs[k], "vrow", axis=1, tiled=True), jnp.int32(0))
        results = term if results is None else results + term
    groups = row_count // col_count
    inner = cols_loc // row_count
    shaped = results[0].reshape(P_SIZE, rows_loc, col_count, groups, 1, inner)
    moved = lax.all_to_all(shaped, "vcol", split_axis=2, concat_axis=4, tiled=True)
    combined = moved.reshape(P_SIZE, rows_loc, cols_loc)
    return combined


MESH = pl.DeviceIdType.MESH
LANES = 128
PAIRS = ((1, 4), (2, 5), (3, 6), (0, 7))
BEHIND = (0, 1, 2, 3, 7)
AHEAD = (0, 4, 5, 6, 7)
FORWARD = ((0, 0), (0, 1), (1, 0), (1, 1), (2, 0), (2, 1), (3, 0))
BACKWARD = ((0, 1), (0, 0), (1, 1), (1, 0), (2, 1), (2, 0), (3, 1))


def ring_place(row):
    y = lax.rem(row // 2, 2)
    z = row // 4
    return z + y * (7 - 2 * z)


def ring_row(place, core):
    y = place // 4
    z = place + y * (7 - 2 * place)
    return z * 4 + y * 2 + core


def ring_kernel(
    own_blocks, sides, natural, turned, gathered, mine, theirs, late,
    rows, piece, factor, totals, weights, sums, came, packed, x_send, x_recv,
    f_send, f_recv, b_send, b_recv, s_send, s_recv, a_send, a_recv, o_send, o_recv, l_sem, p_sem, t_sem,
):
    row = lax.axis_index("vrow")
    col = lax.axis_index("vcol")
    core = lax.rem(row, 2)
    place = ring_place(row)
    right = (ring_row(lax.rem(place + 1, 8), core), col)
    left = (ring_row(lax.rem(place + 7, 8), core), col)
    sibling = (row + 1 - 2 * core, col)
    partner = (row, 1 - col)

    barrier = pltpu.get_barrier_semaphore()
    flips = [sibling, partner]
    for bit in (2, 4, 8):
        flips.append((row + bit - 2 * bit * lax.rem(row // bit, 2), col))
    for other in [right, left] + flips:
        pl.semaphore_signal(barrier, inc=1, device_id=other, device_id_type=MESH)
    pl.semaphore_wait(barrier, 7)

    def remote(src, dst, send, recv, target):
        return pltpu.make_async_remote_copy(
            src_ref=src, dst_ref=dst, send_sem=send, recv_sem=recv, device_id=target, device_id_type=MESH
        )

    def hop(order, slots, send, recv, target, i):
        step, k = order[i]
        src = turned.at[k] if step == 0 else gathered.at[slots[step], core, k]
        return remote(src, gathered.at[slots[step + 1], core, k], send.at[i], recv.at[i], target)

    forward = [hop(FORWARD, BEHIND, f_send, f_recv, right, i) for i in range(7)]
    backward = [hop(BACKWARD, AHEAD, b_send, b_recv, left, i) for i in range(7)]

    def share(slot, k):
        src = turned.at[k] if slot == 0 else gathered.at[slot, core, k]
        return remote(src, gathered.at[slot, core, k], s_send.at[slot, k], s_recv.at[slot, k], sibling)

    shares = {(slot, k): share(slot, k) for slot in range(8) for k in range(2)}
    width = natural.shape[2]
    a_copy = remote(natural, rows.at[:, :, pl.ds(col * width, width), :], a_send, a_recv, partner)
    a_own = pltpu.make_async_copy(natural, rows.at[:, :, pl.ds(col * width, width), :], l_sem.at[0])
    own = pltpu.make_async_copy(turned, gathered.at[0, core], l_sem.at[1])

    forward[0].start()
    backward[0].start()
    sums[0] = own_blocks[...]
    for i, other in enumerate(flips):
        swap = remote(sums.at[i], came.at[i], x_send.at[i], x_recv.at[i], other)
        swap.start()
        swap.wait()
        sums[i + 1] = sums[i] + came[i]

    forward[1].start()
    backward[1].start()
    a_copy.start()
    own.start()
    a_own.start()
    for k in range(2):
        shares[0, k].start()

    ahead = sums[5, 0].astype(jnp.float32)
    mirror = sums[5, 1].astype(jnp.float32)
    full = 0.5 * (ahead + mirror) + 0.5 * (ahead - mirror) * sides[...]
    high = full.astype(jnp.bfloat16)
    weights[:P_SIZE] = high
    weights[P_SIZE:] = (full - high.astype(jnp.float32)).astype(jnp.bfloat16)

    outs = [remote(totals.at[u], theirs.at[u], o_send.at[u], o_recv.at[u], partner) for u in range(3)]
    for h in range(2):
        outs.append(remote(packed.at[h], late.at[h], o_send.at[3 + h], o_recv.at[3 + h], partner))
    send_last = row // 8 == col
    keeps = [pltpu.make_async_copy(totals.at[u], mine.at[u], t_sem.at[u]) for u in range(4)]
    count = rows.shape[2] // BLK
    shard = turned.shape[3]

    def loads_of(u):
        loads = []
        for e, slot in enumerate(PAIRS[u]):
            for c in range(2):
                for k in range(2):
                    dst = piece.at[k, :, :, pl.ds((e * 2 + c) * shard, shard), :]
                    loads.append(pltpu.make_async_copy(gathered.at[slot, c, k], dst, p_sem.at[e, c, k]))
        return loads

    def compute(u, parts):
        part_rows = count // parts

        def products(h, i, carry):
            k = i // 8
            t = lax.rem(i // 4, 2)
            d = lax.rem(i, 4)
            cols = piece[k, 1 - t, pl.ds(d * 2, 2)].reshape(2 * LANES, piece.shape[-1])
            part = lax.dot_general(
                rows[k, t, pl.ds(h * part_rows * BLK, part_rows * BLK)], cols, (((1,), (1,)), ((), ())), preferred_element_type=jnp.float32
            ).reshape(part_rows, BLK, 2 * LANES)
            part = jnp.concatenate([part[:, :, :LANES], part[:, :, LANES:]], axis=1)
            high = part.astype(jnp.bfloat16)
            low = (part - high.astype(jnp.float32)).astype(jnp.bfloat16)
            at = k * 256 + t * 128 + d * 16
            factor[:part_rows, pl.ds(pl.multiple_of(at, 16), 16), :] = high
            factor[:part_rows, pl.ds(pl.multiple_of(at + 64, 16), 16), :] = low
            return carry

        def contract(h, a, carry):
            res = jnp.dot(weights[...], factor[a], preferred_element_type=jnp.float32)
            res = res[:P_SIZE] + res[P_SIZE:]
            totals[u, pl.ds(h * part_rows + a, P_SIZE, stride=count), :] = res
            if u == 3:
                moved = pltpu.roll(res, 64, 1)
                half = P_SIZE // 2
                low = lax.broadcasted_iota(jnp.int32, (half, LANES), 1) < 64
                opposite = jnp.where(low, moved[:half], res[half:])
                near = jnp.where(low, res[:half], moved[half:])
                packed[h, pl.ds(a, half, stride=part_rows), :] = jnp.where(send_last, opposite, near)
            return carry

        for h in range(parts):
            lax.fori_loop(0, 16, functools.partial(products, h), 0)
            lax.fori_loop(0, part_rows, functools.partial(contract, h), 0)
            outs[u + h].start()
        keeps[u].start()

    def sibling_here(slots):
        for slot in slots:
            for k in range(2):
                shares[slot, k].wait_recv()

    for i in range(7):
        forward[i].wait_recv()
        if i + 2 < 7:
            forward[i + 2].start()
        step, k = FORWARD[i]
        shares[BEHIND[step + 1], k].start()
        backward[i].wait_recv()
        if i + 2 < 7:
            backward[i + 2].start()
        step, k = BACKWARD[i]
        shares[AHEAD[step + 1], k].start()
        if i == 1:
            a_own.wait()
            a_copy.wait_recv()
        if i in (1, 3, 5):
            u = i // 2
            sibling_here(PAIRS[u])
            loads = loads_of(u)
            for load in loads:
                load.start()
            for load in loads:
                load.wait()
            compute(u, 1)
        if i == 5:
            own.wait()
            sibling_here((0,))
            loads = loads_of(3)
            for load in loads[:4]:
                load.start()
    sibling_here((7,))
    for load in loads[4:]:
        load.start()
    for load in loads:
        load.wait()
    compute(3, 2)
    for copy in forward + backward + list(shares.values()) + [a_copy]:
        copy.wait_send()
    for copy in keeps + outs:
        copy.wait()


def place_kernel(table, mine, theirs, late, out):
    i = pl.program_id(0)
    last = table[i] == 3
    half = table[4 + i]
    other_half = jnp.where(last, pl.program_id(1) // 2, half)
    swap = table[8]
    shape = out.shape
    a = mine[0].reshape(-1, LANES)
    b = jnp.where(last, jnp.concatenate([late[0], late[1]], axis=1), theirs[0]).reshape(-1, LANES)
    lane = lax.broadcasted_iota(jnp.int32, a.shape, 1)

    def spread(x, source, target):
        shift = target - source + LANES
        return jnp.where(
            lane < 64,
            pltpu.roll(x, lax.rem(shift, LANES), 1),
            pltpu.roll(x, lax.rem(shift + 32, LANES), 1),
        )

    a = spread(a, half * 64, swap * 32)
    b = spread(b, other_half * 64, 32 - swap * 32)
    out[...] = jnp.where(lane // 32 % 2 == swap, a, b).reshape(shape)


def ladder_blocks(pairs, offsets, amplitudes):
    rows_loc, cols_loc = amplitudes.shape[1], amplitudes.shape[2]
    here = lax.axis_index(("vrow", "vcol"))
    col_count = lax.axis_size("vcol")
    zero = jnp.zeros((), jnp.int32)

    def own(first, second):
        block = lax.dynamic_slice(
            amplitudes, (zero, first % rows_loc, second % cols_loc), (P_SIZE, BLK, BLK)
        )
        root = first // rows_loc * col_count + second // cols_loc
        return jnp.where(here == root, block, jnp.zeros_like(block))

    def both(block_cd):
        cd = block_cd.reshape(P_SIZE, BLK * BLK)
        dc = jnp.transpose(block_cd, (0, 2, 1)).reshape(P_SIZE, BLK * BLK)
        return [dc, dc, cd, cd]

    ahead, mirror = [], []
    for k in range(STEPS):
        ahead.extend(both(own(offsets[k, 0], offsets[k, 1])))
        mirror.extend(both(jnp.transpose(own(offsets[k, 1], offsets[k, 0]), (0, 2, 1))))
    blocks = jnp.stack([jnp.concatenate(ahead, axis=1), jnp.concatenate(mirror, axis=1)])
    offdiag = (pairs[:, 0] != pairs[:, 1]).astype(jnp.float32)
    sign = 1.0 - 2.0 * (jnp.arange(blocks.shape[2]) // 128 % 2).astype(jnp.float32)
    return blocks, offdiag[:, None] * sign[None, :]


def on_plane(pairs, offsets, amplitudes, slabs):
    shard, depth = slabs.shape[2], slabs.shape[4]
    rows_loc, cols_loc = amplitudes.shape[1], amplitudes.shape[2]
    own_blocks, sides = ladder_blocks(pairs, offsets, amplitudes)
    natural = slabs.reshape(STEPS, 2, shard * BLK, depth)
    turned = jnp.swapaxes(slabs, 2, 3)
    bf16, f32 = jnp.bfloat16, jnp.float32
    dma = pltpu.SemaphoreType.DMA
    anywhere = pl.BlockSpec(memory_space=pl.ANY)
    _, mine, theirs, late = pl.pallas_call(
        ring_kernel,
        out_shape=(
            jax.ShapeDtypeStruct((8, 2, STEPS, 2, BLK, shard, depth), bf16),
            jax.ShapeDtypeStruct((4, P_SIZE * rows_loc, LANES), f32),
            jax.ShapeDtypeStruct((4, P_SIZE * rows_loc, LANES), f32),
            jax.ShapeDtypeStruct((2, P_SIZE // 2 * rows_loc // 2, LANES), f32),
        ),
        in_specs=[pl.BlockSpec(memory_space=pltpu.VMEM)] * 2 + [anywhere, anywhere],
        out_specs=(anywhere,) * 4,
        scratch_shapes=[
            pltpu.VMEM((STEPS, 2, rows_loc * BLK, depth), bf16),
            pltpu.VMEM((STEPS, 2, BLK, LANES, depth), bf16),
            pltpu.VMEM((rows_loc, STEPS * 256, LANES), bf16),
            pltpu.VMEM((4, P_SIZE * rows_loc, LANES), f32),
            pltpu.VMEM((2 * P_SIZE, STEPS * 256), bf16),
            pltpu.VMEM((6, 2, P_SIZE, STEPS * 256), bf16),
            pltpu.VMEM((5, 2, P_SIZE, STEPS * 256), bf16),
            pltpu.VMEM((2, P_SIZE // 2 * rows_loc // 2, LANES), f32),
            dma((5,)), dma((5,)),
            dma((7,)), dma((7,)), dma((7,)), dma((7,)), dma((8, 2)), dma((8, 2)),
            dma, dma, dma((5,)), dma((5,)), dma((2,)), dma((2, 2, 2)), dma((4,)),
        ],
        compiler_params=pltpu.CompilerParams(
            collective_id=0, has_side_effects=True, vmem_limit_bytes=60 * 1024 * 1024
        ),
        name="ladder_ring",
    )(own_blocks, sides, natural, turned)
    row = lax.axis_index("vrow")
    col = lax.axis_index("vcol")
    chip = jnp.arange(4, dtype=jnp.int32)
    z = 2 * col + chip // 2
    y = chip % 2
    rel = (z + y * (7 - 2 * z) - ring_place(row)) % 8
    block = jnp.array([3, 0, 1, 2, 3, 2, 1, 0], jnp.int32)[rel]
    half = jnp.array([0, 1, 1, 1, 1, 0, 0, 0], jnp.int32)[rel]
    table = jnp.concatenate([block, half, col[None].astype(jnp.int32)])
    chunk = 16
    source = pl.BlockSpec((1, chunk, rows_loc, LANES), lambda i, j, t: (t[i], j, 0, 0))
    other = pl.BlockSpec(
        (1, chunk, rows_loc, LANES), lambda i, j, t: (t[i], jnp.where(t[i] == 3, 0, j), 0, 0)
    )
    final = pl.BlockSpec(
        (2, chunk, rows_loc // 2, LANES), lambda i, j, t: (0, jnp.where(t[i] == 3, j % 2, 0), 0, 0)
    )
    return pl.pallas_call(
        place_kernel,
        grid_spec=pltpu.PrefetchScalarGridSpec(
            num_scalar_prefetch=1,
            grid=(4, P_SIZE // chunk),
            in_specs=[source, other, final],
            out_specs=pl.BlockSpec((chunk, rows_loc, LANES), lambda i, j, t: (j, 0, i)),
        ),
        out_shape=jax.ShapeDtypeStruct((P_SIZE, rows_loc, cols_loc), f32),
        name="ladder_place",
    )(
        table,
        mine.reshape(4, P_SIZE, rows_loc, LANES),
        theirs.reshape(4, P_SIZE, rows_loc, LANES),
        late.reshape(2, P_SIZE // 2, rows_loc // 2, LANES),
    )


def solution(mesh):
    in_specs = (P(), P(), P(None, "vrow", "vcol"), P(None, None, ("vrow", "vcol"), None, None))
    out_specs = P(None, "vrow", "vcol")
    on_slice = on_plane if (mesh.shape["vrow"], mesh.shape["vcol"]) == (16, 2) else on_device
    return jax.shard_map(
        on_slice, mesh=mesh, in_specs=in_specs, out_specs=out_specs, check_vma=False
    )
```

```python
import functools

import jax
import jax.numpy as jnp
from jax import lax
from jax.experimental import pallas as pl
from jax.experimental.pallas import tpu as pltpu
from jax.sharding import PartitionSpec as P

BLK = 8
P_SIZE = 64
STEPS = 2


def broadcast(block, axis, holder):
    block = jnp.where(lax.axis_index(axis) == holder, block, jnp.zeros_like(block))
    return lax.psum(block, axis)


def ladder_part(rows, upper, lower, piece):
    depth = rows.shape[-1]
    count_a = rows.shape[2]
    count_b = piece.shape[2]
    rows_c = rows[0, 0].reshape(count_a * BLK, depth)
    rows_d = rows[0, 1].reshape(count_a * BLK, depth)
    piece_c = piece[0, 0].reshape(count_b * BLK, depth)
    piece_d = piece[0, 1].reshape(count_b * BLK, depth)
    direct = lax.dot_general(
        rows_c, piece_d, (((1,), (1,)), ((), ())), preferred_element_type=jnp.float32
    ).reshape(count_a, BLK, count_b, BLK)
    swapped = lax.dot_general(
        rows_d, piece_c, (((1,), (1,)), ((), ())), preferred_element_type=jnp.float32
    ).reshape(count_a, BLK, count_b, BLK)
    term = jnp.einsum("acbd,pcd->pab", direct, upper[0], precision=lax.Precision.HIGHEST)
    term = term + jnp.einsum("adbc,pcd->pab", swapped, lower[0], precision=lax.Precision.HIGHEST)
    term = term[None]
    return term


def blocks_of(pairs, offsets, amplitudes):
    col_count = lax.axis_size("vcol")
    rows_loc = amplitudes.shape[1]
    cols_loc = amplitudes.shape[2]
    offdiag = (pairs[:, 0] != pairs[:, 1]).astype(jnp.float32)
    zero = jnp.zeros((), jnp.int32)
    upper_list = []
    lower_list = []
    for k in range(STEPS):
        first = offsets[k, 0]
        second = offsets[k, 1]
        own_forward = lax.dynamic_slice(
            amplitudes, (zero, first % rows_loc, second % cols_loc), (P_SIZE, BLK, BLK)
        )
        own_mirror = lax.dynamic_slice(
            amplitudes, (zero, second % rows_loc, first % cols_loc), (P_SIZE, BLK, BLK)
        )
        root_forward = first // rows_loc * col_count + second // cols_loc
        root_mirror = second // rows_loc * col_count + first // cols_loc
        forward = broadcast(own_forward, ("vrow", "vcol"), root_forward).astype(jnp.float32)
        mirror_raw = broadcast(own_mirror, ("vrow", "vcol"), root_mirror).astype(jnp.float32)
        mirror = jnp.transpose(mirror_raw, (0, 2, 1))
        plus = 0.5 * (forward + mirror)
        minus = 0.5 * (forward - mirror) * offdiag[:, None, None]
        upper_list.append(plus + minus)
        lower_list.append(plus - minus)
    return upper_list, lower_list


def on_device(pairs, offsets, amplitudes, slabs):
    row_count = lax.axis_size("vrow")
    col_count = lax.axis_size("vcol")
    rows_loc = amplitudes.shape[1]
    cols_loc = amplitudes.shape[2]
    upper_list, lower_list = blocks_of(pairs, offsets, amplitudes)
    results = None
    for k in range(STEPS):
        rows = lax.all_gather(slabs[k], "vcol", axis=1, tiled=True)

        def single(piece, start, rows=rows, k=k):
            return ladder_part(rows[None], upper_list[k][None], lower_list[k][None], piece[None])

        term = single(lax.all_gather(slabs[k], "vrow", axis=1, tiled=True), jnp.int32(0))
        results = term if results is None else results + term
    groups = row_count // col_count
    inner = cols_loc // row_count
    shaped = results[0].reshape(P_SIZE, rows_loc, col_count, groups, 1, inner)
    moved = lax.all_to_all(shaped, "vcol", split_axis=2, concat_axis=4, tiled=True)
    combined = moved.reshape(P_SIZE, rows_loc, cols_loc)
    return combined


MESH = pl.DeviceIdType.MESH
LANES = 128
PAIRS = ((1, 4), (2, 5), (3, 6), (0, 7))
BEHIND = (0, 1, 2, 3, 7)
AHEAD = (0, 4, 5, 6, 7)
FORWARD = ((0, 0), (0, 1), (1, 0), (1, 1), (2, 0), (2, 1), (3, 0))
BACKWARD = ((0, 1), (0, 0), (1, 1), (1, 0), (2, 1), (2, 0), (3, 1))


def ring_place(row):
    y = lax.rem(row // 2, 2)
    z = row // 4
    return z + y * (7 - 2 * z)


def ring_row(place, core):
    y = place // 4
    z = place + y * (7 - 2 * place)
    return z * 4 + y * 2 + core


def ring_kernel(
    own_blocks, sides, natural, turned, gathered, mine, theirs, late,
    rows, piece, factor, totals, weights, sums, came, packed, x_send, x_recv,
    f_send, f_recv, b_send, b_recv, s_send, s_recv, a_send, a_recv, o_send, o_recv, l_sem, p_sem, t_sem,
):
    row = lax.axis_index("vrow")
    col = lax.axis_index("vcol")
    core = lax.rem(row, 2)
    place = ring_place(row)
    right = (ring_row(lax.rem(place + 1, 8), core), col)
    left = (ring_row(lax.rem(place + 7, 8), core), col)
    sibling = (row + 1 - 2 * core, col)
    partner = (row, 1 - col)

    barrier = pltpu.get_barrier_semaphore()
    flips = [sibling, partner]
    for bit in (2, 4, 8):
        flips.append((row + bit - 2 * bit * lax.rem(row // bit, 2), col))
    for other in [right, left] + flips:
        pl.semaphore_signal(barrier, inc=1, device_id=other, device_id_type=MESH)
    pl.semaphore_wait(barrier, 7)

    def remote(src, dst, send, recv, target):
        return pltpu.make_async_remote_copy(
            src_ref=src, dst_ref=dst, send_sem=send, recv_sem=recv, device_id=target, device_id_type=MESH
        )

    def hop(order, slots, send, recv, target, i):
        step, k = order[i]
        src = turned.at[k] if step == 0 else gathered.at[slots[step], core, k]
        return remote(src, gathered.at[slots[step + 1], core, k], send.at[i], recv.at[i], target)

    forward = [hop(FORWARD, BEHIND, f_send, f_recv, right, i) for i in range(7)]
    backward = [hop(BACKWARD, AHEAD, b_send, b_recv, left, i) for i in range(7)]

    def share(slot, k):
        src = turned.at[k] if slot == 0 else gathered.at[slot, core, k]
        return remote(src, gathered.at[slot, core, k], s_send.at[slot, k], s_recv.at[slot, k], sibling)

    shares = {(slot, k): share(slot, k) for slot in range(8) for k in range(2)}
    width = natural.shape[2]
    a_copy = remote(natural, rows.at[:, :, pl.ds(col * width, width), :], a_send, a_recv, partner)
    a_own = pltpu.make_async_copy(natural, rows.at[:, :, pl.ds(col * width, width), :], l_sem.at[0])
    own = pltpu.make_async_copy(turned, gathered.at[0, core], l_sem.at[1])

    forward[0].start()
    backward[0].start()
    sums[0] = own_blocks[...]
    for i, other in enumerate(flips):
        swap = remote(sums.at[i], came.at[i], x_send.at[i], x_recv.at[i], other)
        swap.start()
        swap.wait()
        sums[i + 1] = sums[i] + came[i]

    forward[1].start()
    backward[1].start()
    a_copy.start()
    own.start()
    a_own.start()
    for k in range(2):
        shares[0, k].start()

    ahead = sums[5, 0].astype(jnp.float32)
    mirror = sums[5, 1].astype(jnp.float32)
    full = 0.5 * (ahead + mirror) + 0.5 * (ahead - mirror) * sides[...]
    high = full.astype(jnp.bfloat16)
    weights[:P_SIZE] = high
    weights[P_SIZE:] = (full - high.astype(jnp.float32)).astype(jnp.bfloat16)

    outs = [remote(totals.at[u], theirs.at[u], o_send.at[u], o_recv.at[u], partner) for u in range(3)]
    for h in range(2):
        outs.append(remote(packed.at[h], late.at[h], o_send.at[3 + h], o_recv.at[3 + h], partner))
    send_last = row // 8 == col
    keeps = [pltpu.make_async_copy(totals.at[u], mine.at[u], t_sem.at[u]) for u in range(4)]
    count = rows.shape[2] // BLK
    shard = turned.shape[3]

    def loads_of(u):
        loads = []
        for e, slot in enumerate(PAIRS[u]):
            for c in range(2):
                for k in range(2):
                    dst = piece.at[k, :, :, pl.ds((e * 2 + c) * shard, shard), :]
                    loads.append(pltpu.make_async_copy(gathered.at[slot, c, k], dst, p_sem.at[e, c, k]))
        return loads

    def compute(u, parts):
        part_rows = count // parts

        def products(h, i, carry):
            k = i // 8
            t = lax.rem(i // 4, 2)
            d = lax.rem(i, 4)
            cols = piece[k, 1 - t, pl.ds(d * 2, 2)].reshape(2 * LANES, piece.shape[-1])
            part = lax.dot_general(
                rows[k, t, pl.ds(h * part_rows * BLK, part_rows * BLK)], cols, (((1,), (1,)), ((), ())), preferred_element_type=jnp.float32
            ).reshape(part_rows, BLK, 2 * LANES)
            part = jnp.concatenate([part[:, :, :LANES], part[:, :, LANES:]], axis=1)
            high = part.astype(jnp.bfloat16)
            low = (part - high.astype(jnp.float32)).astype(jnp.bfloat16)
            at = k * 256 + t * 128 + d * 16
            factor[:part_rows, pl.ds(pl.multiple_of(at, 16), 16), :] = high
            factor[:part_rows, pl.ds(pl.multiple_of(at + 64, 16), 16), :] = low
            return carry

        def contract(h, a, carry):
            res = jnp.dot(weights[...], factor[a], preferred_element_type=jnp.float32)
            res = res[:P_SIZE] + res[P_SIZE:]
            totals[u, pl.ds(h * part_rows + a, P_SIZE, stride=count), :] = res
            if u == 3:
                moved = pltpu.roll(res, 64, 1)
                half = P_SIZE // 2
                low = lax.broadcasted_iota(jnp.int32, (half, LANES), 1) < 64
                opposite = jnp.where(low, moved[:half], res[half:])
                near = jnp.where(low, res[:half], moved[half:])
                packed[h, pl.ds(a, half, stride=part_rows), :] = jnp.where(send_last, opposite, near)
            return carry

        for h in range(parts):
            lax.fori_loop(0, 16, functools.partial(products, h), 0)
            lax.fori_loop(0, part_rows, functools.partial(contract, h), 0, unroll=4)
            outs[u + h].start()
        keeps[u].start()

    def sibling_here(slots):
        for slot in slots:
            for k in range(2):
                shares[slot, k].wait_recv()

    for i in range(7):
        forward[i].wait_recv()
        if i + 2 < 7:
            forward[i + 2].start()
        step, k = FORWARD[i]
        shares[BEHIND[step + 1], k].start()
        backward[i].wait_recv()
        if i + 2 < 7:
            backward[i + 2].start()
        step, k = BACKWARD[i]
        shares[AHEAD[step + 1], k].start()
        if i == 1:
            a_own.wait()
            a_copy.wait_recv()
        if i in (1, 3, 5):
            u = i // 2
            sibling_here(PAIRS[u])
            loads = loads_of(u)
            for load in loads:
                load.start()
            for load in loads:
                load.wait()
            compute(u, 1)
        if i == 5:
            own.wait()
            sibling_here((0,))
            loads = loads_of(3)
            for load in loads[:4]:
                load.start()
    sibling_here((7,))
    for load in loads[4:]:
        load.start()
    for load in loads:
        load.wait()
    compute(3, 2)
    for copy in forward + backward + list(shares.values()) + [a_copy]:
        copy.wait_send()
    for copy in keeps + outs:
        copy.wait()


def place_kernel(table, *refs):
    mine, theirs, late, out = refs[:4], refs[4:8], refs[8], refs[9]
    chunk, rows_loc = out.shape[:2]
    step = pl.program_id(0)
    swap = table[8]
    lane = lax.broadcasted_iota(jnp.int32, (chunk * rows_loc, LANES), 1)
    late_block = jnp.concatenate([late[0], late[1]], axis=1).reshape(-1, LANES)

    def spread(x, source, target):
        shift = target - source + LANES
        return jnp.where(
            lane < 64,
            pltpu.roll(x, lax.rem(shift, LANES), 1),
            pltpu.roll(x, lax.rem(shift + 32, LANES), 1),
        )

    for i in range(4):
        last = table[i] == 3
        half = table[4 + i]
        other_half = jnp.where(last, step // (P_SIZE // chunk // 2), half)
        a = mine[i][0].reshape(-1, LANES)
        b = jnp.where(last, late_block, theirs[i][0].reshape(-1, LANES))
        a = spread(a, half * 64, swap * 32)
        b = spread(b, other_half * 64, 32 - swap * 32)
        block = jnp.where(lane // 32 % 2 == swap, a, b)
        out[:, :, i * LANES : (i + 1) * LANES] = block.reshape(chunk, rows_loc, LANES)


def ladder_blocks(pairs, offsets, amplitudes):
    rows_loc, cols_loc = amplitudes.shape[1], amplitudes.shape[2]
    here = lax.axis_index(("vrow", "vcol"))
    col_count = lax.axis_size("vcol")
    zero = jnp.zeros((), jnp.int32)

    def own(first, second):
        block = lax.dynamic_slice(
            amplitudes, (zero, first % rows_loc, second % cols_loc), (P_SIZE, BLK, BLK)
        )
        root = first // rows_loc * col_count + second // cols_loc
        return jnp.where(here == root, block, jnp.zeros_like(block))

    def both(block_cd):
        cd = block_cd.reshape(P_SIZE, BLK * BLK)
        dc = jnp.transpose(block_cd, (0, 2, 1)).reshape(P_SIZE, BLK * BLK)
        return [dc, dc, cd, cd]

    ahead, mirror = [], []
    for k in range(STEPS):
        ahead.extend(both(own(offsets[k, 0], offsets[k, 1])))
        mirror.extend(both(jnp.transpose(own(offsets[k, 1], offsets[k, 0]), (0, 2, 1))))
    blocks = jnp.stack([jnp.concatenate(ahead, axis=1), jnp.concatenate(mirror, axis=1)])
    offdiag = (pairs[:, 0] != pairs[:, 1]).astype(jnp.float32)
    sign = 1.0 - 2.0 * (jnp.arange(blocks.shape[2]) // 128 % 2).astype(jnp.float32)
    return blocks, offdiag[:, None] * sign[None, :]


def on_plane(pairs, offsets, amplitudes, slabs):
    shard, depth = slabs.shape[2], slabs.shape[4]
    rows_loc, cols_loc = amplitudes.shape[1], amplitudes.shape[2]
    own_blocks, sides = ladder_blocks(pairs, offsets, amplitudes)
    natural = slabs.reshape(STEPS, 2, shard * BLK, depth)
    turned = jnp.swapaxes(slabs, 2, 3)
    bf16, f32 = jnp.bfloat16, jnp.float32
    dma = pltpu.SemaphoreType.DMA
    anywhere = pl.BlockSpec(memory_space=pl.ANY)
    _, mine, theirs, late = pl.pallas_call(
        ring_kernel,
        out_shape=(
            jax.ShapeDtypeStruct((8, 2, STEPS, 2, BLK, shard, depth), bf16),
            jax.ShapeDtypeStruct((4, P_SIZE * rows_loc, LANES), f32),
            jax.ShapeDtypeStruct((4, P_SIZE * rows_loc, LANES), f32),
            jax.ShapeDtypeStruct((2, P_SIZE // 2 * rows_loc // 2, LANES), f32),
        ),
        in_specs=[pl.BlockSpec(memory_space=pltpu.VMEM)] * 2 + [anywhere, anywhere],
        out_specs=(anywhere,) * 4,
        scratch_shapes=[
            pltpu.VMEM((STEPS, 2, rows_loc * BLK, depth), bf16),
            pltpu.VMEM((STEPS, 2, BLK, LANES, depth), bf16),
            pltpu.VMEM((rows_loc, STEPS * 256, LANES), bf16),
            pltpu.VMEM((4, P_SIZE * rows_loc, LANES), f32),
            pltpu.VMEM((2 * P_SIZE, STEPS * 256), bf16),
            pltpu.VMEM((6, 2, P_SIZE, STEPS * 256), bf16),
            pltpu.VMEM((5, 2, P_SIZE, STEPS * 256), bf16),
            pltpu.VMEM((2, P_SIZE // 2 * rows_loc // 2, LANES), f32),
            dma((5,)), dma((5,)),
            dma((7,)), dma((7,)), dma((7,)), dma((7,)), dma((8, 2)), dma((8, 2)),
            dma, dma, dma((5,)), dma((5,)), dma((2,)), dma((2, 2, 2)), dma((4,)),
        ],
        compiler_params=pltpu.CompilerParams(
            collective_id=0, has_side_effects=True, vmem_limit_bytes=60 * 1024 * 1024
        ),
        name="ladder_ring",
    )(own_blocks, sides, natural, turned)
    row = lax.axis_index("vrow")
    col = lax.axis_index("vcol")
    chip = jnp.arange(4, dtype=jnp.int32)
    z = 2 * col + chip // 2
    y = chip % 2
    rel = (z + y * (7 - 2 * z) - ring_place(row)) % 8
    block = jnp.array([3, 0, 1, 2, 3, 2, 1, 0], jnp.int32)[rel]
    half = jnp.array([0, 1, 1, 1, 1, 0, 0, 0], jnp.int32)[rel]
    table = jnp.concatenate([block, half, col[None].astype(jnp.int32)])
    chunk = 8
    steps = P_SIZE // chunk
    shape = (1, chunk, rows_loc, LANES)

    def from_mine(i):
        return pl.BlockSpec(shape, lambda j, t: (t[i], j, 0, 0))

    def from_theirs(i):
        return pl.BlockSpec(shape, lambda j, t: (t[i], jnp.where(t[i] == 3, 0, j), 0, 0))

    final = pl.BlockSpec((2, chunk, rows_loc // 2, LANES), lambda j, t: (0, lax.rem(j, steps // 2), 0, 0))
    mine = mine.reshape(4, P_SIZE, rows_loc, LANES)
    theirs = theirs.reshape(4, P_SIZE, rows_loc, LANES)
    late = late.reshape(2, P_SIZE // 2, rows_loc // 2, LANES)
    return pl.pallas_call(
        place_kernel,
        grid_spec=pltpu.PrefetchScalarGridSpec(
            num_scalar_prefetch=1,
            grid=(steps,),
            in_specs=[from_mine(i) for i in range(4)] + [from_theirs(i) for i in range(4)] + [final],
            out_specs=pl.BlockSpec((chunk, rows_loc, cols_loc), lambda j, t: (j, 0, 0)),
        ),
        out_shape=jax.ShapeDtypeStruct((P_SIZE, rows_loc, cols_loc), f32),
        compiler_params=pltpu.CompilerParams(vmem_limit_bytes=32 * 1024 * 1024),
        name="ladder_place",
    )(table, *[mine] * 4, *[theirs] * 4, late)


def solution(mesh):
    in_specs = (P(), P(), P(None, "vrow", "vcol"), P(None, None, ("vrow", "vcol"), None, None))
    out_specs = P(None, "vrow", "vcol")
    on_slice = on_plane if (mesh.shape["vrow"], mesh.shape["vcol"]) == (16, 2) else on_device
    return jax.shard_map(
        on_slice, mesh=mesh, in_specs=in_specs, out_specs=out_specs, check_vma=False
    )
```

```python
import functools

import jax
import jax.numpy as jnp
from jax import lax
from jax.experimental import pallas as pl
from jax.experimental.pallas import tpu as pltpu
from jax.sharding import PartitionSpec as P

BLK = 8
P_SIZE = 64
STEPS = 2


def broadcast(block, axis, holder):
    block = jnp.where(lax.axis_index(axis) == holder, block, jnp.zeros_like(block))
    return lax.psum(block, axis)


def ladder_part(rows, upper, lower, piece):
    depth = rows.shape[-1]
    count_a = rows.shape[2]
    count_b = piece.shape[2]
    rows_c = rows[0, 0].reshape(count_a * BLK, depth)
    rows_d = rows[0, 1].reshape(count_a * BLK, depth)
    piece_c = piece[0, 0].reshape(count_b * BLK, depth)
    piece_d = piece[0, 1].reshape(count_b * BLK, depth)
    direct = lax.dot_general(
        rows_c, piece_d, (((1,), (1,)), ((), ())), preferred_element_type=jnp.float32
    ).reshape(count_a, BLK, count_b, BLK)
    swapped = lax.dot_general(
        rows_d, piece_c, (((1,), (1,)), ((), ())), preferred_element_type=jnp.float32
    ).reshape(count_a, BLK, count_b, BLK)
    term = jnp.einsum("acbd,pcd->pab", direct, upper[0], precision=lax.Precision.HIGHEST)
    term = term + jnp.einsum("adbc,pcd->pab", swapped, lower[0], precision=lax.Precision.HIGHEST)
    term = term[None]
    return term


def blocks_of(pairs, offsets, amplitudes):
    col_count = lax.axis_size("vcol")
    rows_loc = amplitudes.shape[1]
    cols_loc = amplitudes.shape[2]
    offdiag = (pairs[:, 0] != pairs[:, 1]).astype(jnp.float32)
    zero = jnp.zeros((), jnp.int32)
    upper_list = []
    lower_list = []
    for k in range(STEPS):
        first = offsets[k, 0]
        second = offsets[k, 1]
        own_forward = lax.dynamic_slice(
            amplitudes, (zero, first % rows_loc, second % cols_loc), (P_SIZE, BLK, BLK)
        )
        own_mirror = lax.dynamic_slice(
            amplitudes, (zero, second % rows_loc, first % cols_loc), (P_SIZE, BLK, BLK)
        )
        root_forward = first // rows_loc * col_count + second // cols_loc
        root_mirror = second // rows_loc * col_count + first // cols_loc
        forward = broadcast(own_forward, ("vrow", "vcol"), root_forward).astype(jnp.float32)
        mirror_raw = broadcast(own_mirror, ("vrow", "vcol"), root_mirror).astype(jnp.float32)
        mirror = jnp.transpose(mirror_raw, (0, 2, 1))
        plus = 0.5 * (forward + mirror)
        minus = 0.5 * (forward - mirror) * offdiag[:, None, None]
        upper_list.append(plus + minus)
        lower_list.append(plus - minus)
    return upper_list, lower_list


def on_device(pairs, offsets, amplitudes, slabs):
    row_count = lax.axis_size("vrow")
    col_count = lax.axis_size("vcol")
    rows_loc = amplitudes.shape[1]
    cols_loc = amplitudes.shape[2]
    upper_list, lower_list = blocks_of(pairs, offsets, amplitudes)
    results = None
    for k in range(STEPS):
        rows = lax.all_gather(slabs[k], "vcol", axis=1, tiled=True)

        def single(piece, start, rows=rows, k=k):
            return ladder_part(rows[None], upper_list[k][None], lower_list[k][None], piece[None])

        term = single(lax.all_gather(slabs[k], "vrow", axis=1, tiled=True), jnp.int32(0))
        results = term if results is None else results + term
    groups = row_count // col_count
    inner = cols_loc // row_count
    shaped = results[0].reshape(P_SIZE, rows_loc, col_count, groups, 1, inner)
    moved = lax.all_to_all(shaped, "vcol", split_axis=2, concat_axis=4, tiled=True)
    combined = moved.reshape(P_SIZE, rows_loc, cols_loc)
    return combined


MESH = pl.DeviceIdType.MESH
LANES = 128
PAIRS = ((1, 4), (2, 5), (3, 6), (0, 7))
BEHIND = (0, 1, 2, 3, 7)
AHEAD = (0, 4, 5, 6, 7)
FORWARD = ((0, 0), (0, 1), (1, 0), (1, 1), (2, 0), (2, 1), (3, 0))
BACKWARD = ((0, 1), (0, 0), (1, 1), (1, 0), (2, 1), (2, 0), (3, 1))


def ring_place(row):
    y = lax.rem(row // 2, 2)
    z = row // 4
    return z + y * (7 - 2 * z)


def ring_row(place, core):
    y = place // 4
    z = place + y * (7 - 2 * place)
    return z * 4 + y * 2 + core


def ring_kernel(
    own_blocks, sides, natural, turned, gathered, mine, theirs, late,
    rows, piece, factor, totals, weights, sums, came, packed, x_send, x_recv,
    f_send, f_recv, b_send, b_recv, s_send, s_recv, a_send, a_recv, o_send, o_recv, l_sem, p_sem, t_sem,
):
    row = lax.axis_index("vrow")
    col = lax.axis_index("vcol")
    core = lax.rem(row, 2)
    place = ring_place(row)
    right = (ring_row(lax.rem(place + 1, 8), core), col)
    left = (ring_row(lax.rem(place + 7, 8), core), col)
    sibling = (row + 1 - 2 * core, col)
    partner = (row, 1 - col)

    barrier = pltpu.get_barrier_semaphore()
    flips = [sibling, partner]
    for bit in (2, 4, 8):
        flips.append((row + bit - 2 * bit * lax.rem(row // bit, 2), col))
    for other in [right, left] + flips:
        pl.semaphore_signal(barrier, inc=1, device_id=other, device_id_type=MESH)
    pl.semaphore_wait(barrier, 7)

    def remote(src, dst, send, recv, target):
        return pltpu.make_async_remote_copy(
            src_ref=src, dst_ref=dst, send_sem=send, recv_sem=recv, device_id=target, device_id_type=MESH
        )

    def hop(order, slots, send, recv, target, i):
        step, k = order[i]
        src = turned.at[k] if step == 0 else gathered.at[slots[step], core, k]
        return remote(src, gathered.at[slots[step + 1], core, k], send.at[i], recv.at[i], target)

    forward = [hop(FORWARD, BEHIND, f_send, f_recv, right, i) for i in range(7)]
    backward = [hop(BACKWARD, AHEAD, b_send, b_recv, left, i) for i in range(7)]

    def share(slot, k):
        src = turned.at[k] if slot == 0 else gathered.at[slot, core, k]
        return remote(src, gathered.at[slot, core, k], s_send.at[slot, k], s_recv.at[slot, k], sibling)

    shares = {(slot, k): share(slot, k) for slot in range(8) for k in range(2)}
    width = natural.shape[2]
    a_copy = remote(natural, rows.at[:, :, pl.ds(col * width, width), :], a_send, a_recv, partner)
    a_own = pltpu.make_async_copy(natural, rows.at[:, :, pl.ds(col * width, width), :], l_sem.at[0])
    own = pltpu.make_async_copy(turned, gathered.at[0, core], l_sem.at[1])

    forward[0].start()
    backward[0].start()
    sums[0] = own_blocks[...]
    for i, other in enumerate(flips):
        swap = remote(sums.at[i], came.at[i], x_send.at[i], x_recv.at[i], other)
        swap.start()
        swap.wait()
        sums[i + 1] = sums[i] + came[i]

    forward[1].start()
    backward[1].start()
    a_copy.start()
    own.start()
    a_own.start()
    for k in range(2):
        shares[0, k].start()

    ahead = sums[5, 0].astype(jnp.float32)
    mirror = sums[5, 1].astype(jnp.float32)
    full = 0.5 * (ahead + mirror) + 0.5 * (ahead - mirror) * sides[...]
    high = full.astype(jnp.bfloat16)
    weights[:P_SIZE] = high
    weights[P_SIZE:] = (full - high.astype(jnp.float32)).astype(jnp.bfloat16)

    outs = [remote(totals.at[u], theirs.at[u], o_send.at[u], o_recv.at[u], partner) for u in range(3)]
    for h in range(2):
        outs.append(remote(packed.at[h], late.at[h], o_send.at[3 + h], o_recv.at[3 + h], partner))
    send_last = row // 8 == col
    keeps = [pltpu.make_async_copy(totals.at[u], mine.at[u], t_sem.at[u]) for u in range(4)]
    count = rows.shape[2] // BLK
    shard = turned.shape[3]

    def loads_of(u):
        loads = []
        for e, slot in enumerate(PAIRS[u]):
            for c in range(2):
                for k in range(2):
                    dst = piece.at[k, :, :, pl.ds((e * 2 + c) * shard, shard), :]
                    loads.append(pltpu.make_async_copy(gathered.at[slot, c, k], dst, p_sem.at[e, c, k]))
        return loads

    def compute(u, parts):
        part_rows = count // parts

        def products(h, i, carry):
            k = i // 8
            t = lax.rem(i // 4, 2)
            d = lax.rem(i, 4)
            cols = piece[k, 1 - t, pl.ds(d * 2, 2)].reshape(2 * LANES, piece.shape[-1])
            part = lax.dot_general(
                rows[k, t, pl.ds(h * part_rows * BLK, part_rows * BLK)], cols, (((1,), (1,)), ((), ())), preferred_element_type=jnp.float32
            ).reshape(part_rows, BLK, 2 * LANES)
            part = jnp.concatenate([part[:, :, :LANES], part[:, :, LANES:]], axis=1)
            high = part.astype(jnp.bfloat16)
            low = (part - high.astype(jnp.float32)).astype(jnp.bfloat16)
            at = k * 256 + t * 128 + d * 16
            factor[:part_rows, pl.ds(pl.multiple_of(at, 16), 16), :] = high
            factor[:part_rows, pl.ds(pl.multiple_of(at + 64, 16), 16), :] = low
            return carry

        def contract(h, a, carry):
            res = jnp.dot(weights[...], factor[a], preferred_element_type=jnp.float32)
            res = res[:P_SIZE] + res[P_SIZE:]
            totals[u, pl.ds(h * part_rows + a, P_SIZE, stride=count), :] = res
            if u == 3:
                moved = pltpu.roll(res, 64, 1)
                half = P_SIZE // 2
                low = lax.broadcasted_iota(jnp.int32, (half, LANES), 1) < 64
                opposite = jnp.where(low, moved[:half], res[half:])
                near = jnp.where(low, res[:half], moved[half:])
                packed[h, pl.ds(a, half, stride=part_rows), :] = jnp.where(send_last, opposite, near)
            return carry

        for h in range(parts):
            lax.fori_loop(0, 16, functools.partial(products, h), 0, unroll=2)
            lax.fori_loop(0, part_rows, functools.partial(contract, h), 0, unroll=8)
            outs[u + h].start()
        keeps[u].start()

    def sibling_here(slots):
        for slot in slots:
            for k in range(2):
                shares[slot, k].wait_recv()

    for i in range(7):
        forward[i].wait_recv()
        if i + 2 < 7:
            forward[i + 2].start()
        step, k = FORWARD[i]
        shares[BEHIND[step + 1], k].start()
        backward[i].wait_recv()
        if i + 2 < 7:
            backward[i + 2].start()
        step, k = BACKWARD[i]
        shares[AHEAD[step + 1], k].start()
        if i == 1:
            a_own.wait()
            a_copy.wait_recv()
        if i in (1, 3, 5):
            u = i // 2
            sibling_here(PAIRS[u])
            loads = loads_of(u)
            for load in loads:
                load.start()
            for load in loads:
                load.wait()
            compute(u, 1)
        if i == 5:
            own.wait()
            sibling_here((0,))
            loads = loads_of(3)
            for load in loads[:4]:
                load.start()
    sibling_here((7,))
    for load in loads[4:]:
        load.start()
    for load in loads:
        load.wait()
    compute(3, 2)
    for copy in forward + backward + list(shares.values()) + [a_copy]:
        copy.wait_send()
    for copy in keeps + outs:
        copy.wait()


def place_kernel(table, *refs):
    mine, theirs, late, out = refs[:4], refs[4:8], refs[8], refs[9]
    chunk, rows_loc = out.shape[:2]
    step = pl.program_id(0)
    swap = table[8]
    lane = lax.broadcasted_iota(jnp.int32, (chunk * rows_loc, LANES), 1)
    late_block = jnp.concatenate([late[0], late[1]], axis=1).reshape(-1, LANES)

    def spread(x, source, target):
        shift = target - source + LANES
        return jnp.where(
            lane < 64,
            pltpu.roll(x, lax.rem(shift, LANES), 1),
            pltpu.roll(x, lax.rem(shift + 32, LANES), 1),
        )

    for i in range(4):
        last = table[i] == 3
        half = table[4 + i]
        other_half = jnp.where(last, step // (P_SIZE // chunk // 2), half)
        a = mine[i][0].reshape(-1, LANES)
        b = jnp.where(last, late_block, theirs[i][0].reshape(-1, LANES))
        a = spread(a, half * 64, swap * 32)
        b = spread(b, other_half * 64, 32 - swap * 32)
        block = jnp.where(lane // 32 % 2 == swap, a, b)
        out[:, :, i * LANES : (i + 1) * LANES] = block.reshape(chunk, rows_loc, LANES)


def ladder_blocks(pairs, offsets, amplitudes):
    rows_loc, cols_loc = amplitudes.shape[1], amplitudes.shape[2]
    here = lax.axis_index(("vrow", "vcol"))
    col_count = lax.axis_size("vcol")
    zero = jnp.zeros((), jnp.int32)

    def own(first, second):
        block = lax.dynamic_slice(
            amplitudes, (zero, first % rows_loc, second % cols_loc), (P_SIZE, BLK, BLK)
        )
        root = first // rows_loc * col_count + second // cols_loc
        return jnp.where(here == root, block, jnp.zeros_like(block))

    def both(block_cd):
        cd = block_cd.reshape(P_SIZE, BLK * BLK)
        dc = jnp.transpose(block_cd, (0, 2, 1)).reshape(P_SIZE, BLK * BLK)
        return [dc, dc, cd, cd]

    ahead, mirror = [], []
    for k in range(STEPS):
        ahead.extend(both(own(offsets[k, 0], offsets[k, 1])))
        mirror.extend(both(jnp.transpose(own(offsets[k, 1], offsets[k, 0]), (0, 2, 1))))
    blocks = jnp.stack([jnp.concatenate(ahead, axis=1), jnp.concatenate(mirror, axis=1)])
    offdiag = (pairs[:, 0] != pairs[:, 1]).astype(jnp.float32)
    sign = 1.0 - 2.0 * (jnp.arange(blocks.shape[2]) // 128 % 2).astype(jnp.float32)
    return blocks, offdiag[:, None] * sign[None, :]


def on_plane(pairs, offsets, amplitudes, slabs):
    shard, depth = slabs.shape[2], slabs.shape[4]
    rows_loc, cols_loc = amplitudes.shape[1], amplitudes.shape[2]
    own_blocks, sides = ladder_blocks(pairs, offsets, amplitudes)
    natural = slabs.reshape(STEPS, 2, shard * BLK, depth)
    turned = jnp.swapaxes(slabs, 2, 3)
    bf16, f32 = jnp.bfloat16, jnp.float32
    dma = pltpu.SemaphoreType.DMA
    anywhere = pl.BlockSpec(memory_space=pl.ANY)
    _, mine, theirs, late = pl.pallas_call(
        ring_kernel,
        out_shape=(
            jax.ShapeDtypeStruct((8, 2, STEPS, 2, BLK, shard, depth), bf16),
            jax.ShapeDtypeStruct((4, P_SIZE * rows_loc, LANES), f32),
            jax.ShapeDtypeStruct((4, P_SIZE * rows_loc, LANES), f32),
            jax.ShapeDtypeStruct((2, P_SIZE // 2 * rows_loc // 2, LANES), f32),
        ),
        in_specs=[pl.BlockSpec(memory_space=pltpu.VMEM)] * 2 + [anywhere, anywhere],
        out_specs=(anywhere,) * 4,
        scratch_shapes=[
            pltpu.VMEM((STEPS, 2, rows_loc * BLK, depth), bf16),
            pltpu.VMEM((STEPS, 2, BLK, LANES, depth), bf16),
            pltpu.VMEM((rows_loc, STEPS * 256, LANES), bf16),
            pltpu.VMEM((4, P_SIZE * rows_loc, LANES), f32),
            pltpu.VMEM((2 * P_SIZE, STEPS * 256), bf16),
            pltpu.VMEM((6, 2, P_SIZE, STEPS * 256), bf16),
            pltpu.VMEM((5, 2, P_SIZE, STEPS * 256), bf16),
            pltpu.VMEM((2, P_SIZE // 2 * rows_loc // 2, LANES), f32),
            dma((5,)), dma((5,)),
            dma((7,)), dma((7,)), dma((7,)), dma((7,)), dma((8, 2)), dma((8, 2)),
            dma, dma, dma((5,)), dma((5,)), dma((2,)), dma((2, 2, 2)), dma((4,)),
        ],
        compiler_params=pltpu.CompilerParams(
            collective_id=0, has_side_effects=True, vmem_limit_bytes=60 * 1024 * 1024
        ),
        name="ladder_ring",
    )(own_blocks, sides, natural, turned)
    row = lax.axis_index("vrow")
    col = lax.axis_index("vcol")
    chip = jnp.arange(4, dtype=jnp.int32)
    z = 2 * col + chip // 2
    y = chip % 2
    rel = (z + y * (7 - 2 * z) - ring_place(row)) % 8
    block = jnp.array([3, 0, 1, 2, 3, 2, 1, 0], jnp.int32)[rel]
    half = jnp.array([0, 1, 1, 1, 1, 0, 0, 0], jnp.int32)[rel]
    table = jnp.concatenate([block, half, col[None].astype(jnp.int32)])
    chunk = 8
    steps = P_SIZE // chunk
    shape = (1, chunk, rows_loc, LANES)

    def from_mine(i):
        return pl.BlockSpec(shape, lambda j, t: (t[i], j, 0, 0))

    def from_theirs(i):
        return pl.BlockSpec(shape, lambda j, t: (t[i], jnp.where(t[i] == 3, 0, j), 0, 0))

    final = pl.BlockSpec((2, chunk, rows_loc // 2, LANES), lambda j, t: (0, lax.rem(j, steps // 2), 0, 0))
    mine = mine.reshape(4, P_SIZE, rows_loc, LANES)
    theirs = theirs.reshape(4, P_SIZE, rows_loc, LANES)
    late = late.reshape(2, P_SIZE // 2, rows_loc // 2, LANES)
    return pl.pallas_call(
        place_kernel,
        grid_spec=pltpu.PrefetchScalarGridSpec(
            num_scalar_prefetch=1,
            grid=(steps,),
            in_specs=[from_mine(i) for i in range(4)] + [from_theirs(i) for i in range(4)] + [final],
            out_specs=pl.BlockSpec((chunk, rows_loc, cols_loc), lambda j, t: (j, 0, 0)),
        ),
        out_shape=jax.ShapeDtypeStruct((P_SIZE, rows_loc, cols_loc), f32),
        compiler_params=pltpu.CompilerParams(vmem_limit_bytes=32 * 1024 * 1024),
        name="ladder_place",
    )(table, *[mine] * 4, *[theirs] * 4, late)


def solution(mesh):
    in_specs = (P(), P(), P(None, "vrow", "vcol"), P(None, None, ("vrow", "vcol"), None, None))
    out_specs = P(None, "vrow", "vcol")
    on_slice = on_plane if (mesh.shape["vrow"], mesh.shape["vcol"]) == (16, 2) else on_device
    return jax.shard_map(
        on_slice, mesh=mesh, in_specs=in_specs, out_specs=out_specs, check_vma=False
    )
```
